32 devices in a mesh: lon: 8 (over y, x, core), lat: 4 (over z).
Axes of the slice: x: 2, y: 2, z: 4, core: 2. Of those that a mesh axis runs over, the one named last changes fastest.
Arguments:
- direction: float32 [75, 32, 1024], P(None, 'lat', 'lon'), may hold values from -40 to 40
- residual: float32 [75, 32, 1024], P(None, 'lat', 'lon'), may hold values from -40 to 40
- eof_basis: float32 [75, 75], replicated, may hold values from -0.75 to 0.75
- kappa_east: float32 [32, 1024], P('lat', 'lon'), may hold values from 0.02 to 0.24
- kappa_north: float32 [32, 1024], P('lat', 'lon'), may hold values from 0.02 to 0.24
- wet_mask: int32 [32, 1024], P('lat', 'lon'), may hold values 0 or 1
- obs_base: int32 [4, 8, 256], P('lat', 'lon'), may hold values from 0 to 1023, as said below
- obs_frac: float32 [2, 4, 8, 256], P(None, 'lat', 'lon'), may hold values from 0 to 1
- obs_rinv: float32 [75, 4, 8, 256], P(None, 'lat', 'lon'), may hold values from 0.25 to 4
Outputs:
- new_residual: float32 [75, 32, 1024], P(None, 'lat', 'lon')
- new_direction: float32 [75, 32, 1024], P(None, 'lat', 'lon')
- step_length: float32 [], replicated
The draws below stay inside these ranges and needn't reach their ends.
Inputs may be any that keep to these rules, and one draw needn't show every extreme that they name: `obs_base`: s // 128 and s % 128 are the row and column of the square's south-west cell within the tile; no profile of the top tile row has its south-west cell in the grid's top row.
All inputs are finite; a program needn't handle non-finite values. No bound on the sum of `wet_mask` on one device may be relied on, other than what follows from the above.
Results may differ from the reference program's by a relative error of at most 0.000066.
Values sent between devices are 32-bit elements; how exact they have to be, the bound alone decides.
A program may use at most 64 MiB of HBM per device.

```python
import math
from functools import partial
import jax
import jax.numpy as jnp
from jax import lax

K = 75
CLAT = 8
CLON = 128
OBS_DEV = 256
NLAT = 32
NLON = 1024
N_LON = 8
N_LAT = 4


def scaled_field(key, stream_id):
    key_main = jax.random.fold_in(key, stream_id)
    key_a, key_b = jax.random.split(key_main)
    lat_pos = jnp.arange(NLAT, dtype=jnp.float32) / max(NLAT - 1, 1)
    lon_pos = jnp.arange(NLON, dtype=jnp.float32) / max(NLON - 1, 1)
    random_part = jax.random.truncated_normal(key_a, -4.0, 4.0, (K, NLAT, NLON), jnp.float32)
    trend_exp = 0.5 * (lat_pos[:, None] + lon_pos[None, :]) - 0.5
    level_scale = 10.0 ** (jax.random.uniform(key_b, (K,), jnp.float32) - 0.5)
    return random_part * level_scale[:, None, None] * (10.0 ** trend_exp)[None]


def draw_direction(key, part):
    return scaled_field(key, 11)


def draw_residual(key, part):
    return scaled_field(key, 23)


def draw_obs_base(key, part):
    key_row, key_col = jax.random.split(jax.random.fold_in(key, 7))
    tiles_lat = NLAT // CLAT
    tiles_lon = NLON // CLON
    out_shape = (tiles_lat, tiles_lon, OBS_DEV)
    top_tile = jnp.arange(tiles_lat, dtype=jnp.int32)[:, None, None] == tiles_lat - 1
    row_limit = jnp.broadcast_to(jnp.where(top_tile, CLAT - 1, CLAT), out_shape).astype(jnp.int32)
    rows_drawn = jax.random.randint(key_row, out_shape, 0, row_limit, dtype=jnp.int32)
    cols_drawn = jax.random.randint(key_col, out_shape, 0, CLON, dtype=jnp.int32)
    base_cells = rows_drawn * CLON + cols_drawn
    base_cells = base_cells.at[0, 0, 0].set(CLAT * CLON - 1)
    return base_cells.at[0, 0, 1].set(0)


def plant(drawn, own_key, low, largest):
    longest = drawn.shape.index(max(drawn.shape))
    spots = []
    for shift in (0, 1):
        where = [jax.random.randint(jax.random.fold_in(own_key, axis), (), 0, length) for axis, length in enumerate(drawn.shape)]
        where[longest] = (where[longest] + shift) % drawn.shape[longest]
        spots.append(tuple(where))
    return drawn.at[spots[0]].set(low).at[spots[1]].set(largest)


def shard_levels(own_key, dims, cuts, smallest, high):
    factor_of, own = 1.0, jax.random.fold_in(own_key, 6)
    for position, shards_of in cuts:
        draws = jnp.exp(jax.random.uniform(jax.random.fold_in(own, position), (shards_of,), jnp.float32, smallest / len(cuts), high / len(cuts)))
        factor_of = factor_of * jnp.repeat(draws, dims[position] // shards_of).reshape([-1 if axis == position else 1 for axis in range(len(dims))])
    return factor_of


def gaussian(own_key, dims, spread, reach, held_as=jnp.bfloat16):
    return jnp.clip(spread * jax.random.normal(own_key, dims, jnp.float32), -reach, reach).astype(held_as)


def setup_inputs(seed: int = 0) -> dict:
    streams_of = jax.random.split(jax.random.key(seed), 10)
    direction = draw_direction(jax.random.fold_in(streams_of[9], 71), 0)
    residual = draw_residual(jax.random.fold_in(streams_of[9], 71), 0)
    eof_basis = gaussian(streams_of[2], (K, K), K ** -0.5, 0.75, jnp.float32)
    kappa_east = jnp.clip(jnp.exp(math.log(0.24) - 2.4849066 * jax.random.uniform(streams_of[3], (NLAT, NLON), jnp.float32) ** shard_levels(streams_of[3], (NLAT, NLON), ((0, 4), (1, 8)), -0.2, 0.2)), 0.02, 0.24)
    kappa_north = jnp.clip(jnp.exp(math.log(0.24) - 2.4849066 * jax.random.uniform(streams_of[4], (NLAT, NLON), jnp.float32) ** shard_levels(streams_of[4], (NLAT, NLON), ((0, 4), (1, 8)), -0.2, 0.2)), 0.02, 0.24)
    wet_mask = plant((jax.random.randint(streams_of[5], (NLAT, NLON), 0, 5) < 4).astype(jnp.int32), jax.random.fold_in(streams_of[5], 1), 0, 1)
    obs_base = draw_obs_base(jax.random.fold_in(streams_of[9], 71), 0)
    obs_frac = jnp.clip(1.0 * jax.random.uniform(streams_of[7], (2, N_LAT, N_LON, OBS_DEV), jnp.float32) ** shard_levels(streams_of[7], (2, N_LAT, N_LON, OBS_DEV), ((1, 4), (2, 8)), -0.2, 0.2), 0.0, 1.0)
    obs_rinv = jnp.clip(jnp.exp(math.log(4.0) - 2.7725887 * jax.random.uniform(streams_of[8], (K, N_LAT, N_LON, OBS_DEV), jnp.float32) ** shard_levels(streams_of[8], (K, N_LAT, N_LON, OBS_DEV), ((1, 4), (2, 8)), -0.2, 0.2)), 0.25, 4.0)
    return dict(direction=direction, residual=residual, eof_basis=eof_basis, kappa_east=kappa_east, kappa_north=kappa_north, wet_mask=wet_mask, obs_base=obs_base, obs_frac=obs_frac, obs_rinv=obs_rinv)


def three_steps(plane, east_face, north_face, fold_face):
    west_face = jnp.roll(east_face, 1, axis=1)
    south_face = jnp.concatenate([jnp.zeros_like(north_face[:1]), north_face[:-1]], 0)
    for step_index in range(3):
        zero_line = jnp.zeros_like(plane[:1])
        north_vals = jnp.concatenate([plane[1:], zero_line], 0)
        south_vals = jnp.concatenate([zero_line, plane[:-1]], 0)
        change = east_face * (jnp.roll(plane, -1, axis=1) - plane)
        change = change + west_face * (jnp.roll(plane, 1, axis=1) - plane)
        change = change + north_face * (north_vals - plane) + south_face * (south_vals - plane)
        change = change.at[-1].add(fold_face * (plane[-1, ::-1] - plane[-1]))
        plane = plane + change
    return plane


def reference(direction, residual, eof_basis, kappa_east, kappa_north, wet_mask, obs_base, obs_frac, obs_rinv):
    wet_float = wet_mask.astype(jnp.float32)
    east_face = kappa_east * wet_float * jnp.roll(wet_float, -1, axis=1)
    wet_above = jnp.concatenate([wet_float[1:], jnp.zeros_like(wet_float[:1])], 0)
    north_face = kappa_north * wet_float * wet_above
    fold_face = 0.5 * (kappa_north[-1] + kappa_north[-1, ::-1]) * wet_float[-1] * wet_float[-1, ::-1]
    diffuse_all = partial(three_steps, east_face=east_face, north_face=north_face, fold_face=fold_face)

    control = direction.reshape(K, -1)
    physical = jnp.dot(eof_basis, control, precision=lax.Precision.HIGHEST, preferred_element_type=jnp.float32)
    physical = lax.map(diffuse_all, physical.reshape(K, NLAT, NLON))
    flat_field = physical.reshape(K, -1)

    row_in = obs_base // CLON
    col_in = obs_base % CLON
    tile_lat = jnp.arange(N_LAT, dtype=jnp.int32)[:, None, None]
    tile_lon = jnp.arange(N_LON, dtype=jnp.int32)[None, :, None]
    glob_row = (tile_lat * CLAT + row_in).reshape(-1)
    glob_col = (tile_lon * CLON + col_in).reshape(-1)
    next_col = (glob_col + 1) % NLON
    corner_index = (glob_row * NLON + glob_col, glob_row * NLON + next_col,
                    (glob_row + 1) * NLON + glob_col, (glob_row + 1) * NLON + next_col)
    lat_frac = obs_frac[0].reshape(-1)
    lon_frac = obs_frac[1].reshape(-1)
    corner_weight = ((1.0 - lat_frac) * (1.0 - lon_frac), (1.0 - lat_frac) * lon_frac,
                     lat_frac * (1.0 - lon_frac), lat_frac * lon_frac)
    profiles = jnp.zeros((K, lat_frac.shape[0]), jnp.float32)
    for corner in range(4):
        profiles = profiles + corner_weight[corner][None, :] * flat_field[:, corner_index[corner]]
    weighted = obs_rinv.reshape(K, -1) * profiles
    adjoint = jnp.zeros((K, NLAT * NLON), jnp.float32)
    for corner in range(4):
        adjoint = adjoint.at[:, corner_index[corner]].add(corner_weight[corner][None, :] * weighted)
    adjoint = lax.map(diffuse_all, adjoint.reshape(K, NLAT, NLON))
    back = jnp.dot(eof_basis.T, adjoint.reshape(K, -1), precision=lax.Precision.HIGHEST, preferred_element_type=jnp.float32)
    image = direction + back.reshape(K, NLAT, NLON)

    old_norm = jnp.sum(residual * residual)
    curvature = jnp.sum(direction * image)
    step_length = old_norm / curvature
    new_residual = residual - step_length * image
    new_norm = jnp.sum(new_residual * new_residual)
    new_direction = new_residual + (new_norm / old_norm) * direction
    return new_residual, new_direction, step_length
```

```python
import jax
import jax.numpy as jnp
from jax import lax
from jax.experimental import pallas as pl
from jax.experimental.pallas import tpu as pltpu
from jax.sharding import PartitionSpec as P

F32 = jnp.float32
MESH = pl.DeviceIdType.MESH


def mm(a, b, dims=((1,), (0,))):
    return lax.dot_general(
        a, b, (dims, ((), ())), precision=lax.Precision.HIGHEST, preferred_element_type=F32
    )


def make_kernel(n_lon, n_lat, levels, rows, width, n_obs):
    padded_levels = -(-(levels + 3) // 8) * 8
    lp = padded_levels
    ke_at, kn_at, wet_at = levels, levels + 1, levels + 2
    first = 4
    top_slot = first + rows - 1
    after = first + rows

    def roll(x, shift):
        shift = shift % width
        return x if shift == 0 else pltpu.roll(x, shift, 1)

    def kernel(
        d_ref, r_ref, eof_ref, ke_ref, kn_ref, wet_ref, base_ref, frac_ref, rinv_ref,
        nr_ref, nd_ref, step_ref,
        field_a, field_b, halo_a, halo_b, coef, hcoef,
        pack_a, east_a, west_a, comb_a, flip_a, flipc_a, north_a, south_a, cnorth_a, csouth_a,
        spread, pack_b, east_b, west_b, comb_b, flip_b, flipc_b, north_b, south_b, cnorth_b, csouth_b,
        eof_pad, rinv_pad, image, red, lon_in, red2, lat_in,
        send_sem, recv_sem, lon_send, lon_recv, lat_send, lat_recv,
    ):
        lon = lax.axis_index("lon")
        lat = lax.axis_index("lat")
        is_top = lat == n_lat - 1
        is_bottom = lat == 0
        east = (lax.rem(lon + 1, n_lon), lat)
        west = (lax.rem(lon + n_lon - 1, n_lon), lat)
        mirror = (n_lon - 1 - lon, lat)
        north = (lon, lax.rem(lat + 1, n_lat))
        south = (lon, lax.rem(lat + n_lat - 1, n_lat))
        lane = lax.broadcasted_iota(jnp.int32, (lp, width), 1)
        lane1 = lane[:1]
        sub8 = lax.rem(lane, 8)

        barrier = pltpu.get_barrier_semaphore()
        for k in range(1, n_lon):
            pl.semaphore_signal(barrier, inc=1, device_id=(lax.rem(lon + k, n_lon), lat), device_id_type=MESH)
        for k in range(1, n_lat):
            pl.semaphore_signal(barrier, inc=1, device_id=(lon, lax.rem(lat + k, n_lat)), device_id_type=MESH)

        for j in range(rows):
            e = first + j
            field_a[e, 0:levels, :] = d_ref[:, j, :]
            field_a[e, ke_at : ke_at + 1, :] = ke_ref[j : j + 1, :]
            field_a[e, kn_at : kn_at + 1, :] = kn_ref[j : j + 1, :]
            field_a[e, wet_at : wet_at + 1, :] = wet_ref[j : j + 1, :].astype(F32)
            if lp > levels + 3:
                field_a[e, levels + 3 : lp, :] = jnp.zeros((lp - levels - 3, width), F32)

        def group(e):
            off = lane - e * 8
            return (off >= -4) & (off < 4)

        def packed(ref, slots, shift=0):
            out = jnp.zeros((lp, width), F32)
            for e in slots:
                out = jnp.where(group(e), roll(ref[e - shift], e * 8), out)
            return out

        row_id = lax.broadcasted_iota(jnp.int32, (width, width), 0)
        col_id = lax.broadcasted_iota(jnp.int32, (width, width), 1)
        reverse = (row_id + col_id == width - 1).astype(F32)

        def flip(x):
            return mm(x, reverse)

        def flip_packed(x):
            return roll(mm(x, reverse), (2 * top_slot + 1) * 8 - 64 - width)

        def remote(src, dst, index, device):
            return pltpu.make_async_remote_copy(
                src_ref=src, dst_ref=dst, send_sem=send_sem.at[index], recv_sem=recv_sem.at[index],
                device_id=device, device_id_type=MESH,
            )

        pack_a[...] = packed(field_a, range(first, after))
        pl.semaphore_wait(barrier, n_lon + n_lat - 2)

        to_west = remote(pack_a, east_a, 0, west)
        to_east = remote(pack_a, west_a, 1, east)
        to_west.start()
        to_east.start()
        to_north = remote(field_a.at[pl.ds(after - 3, 3)], south_a, 2, north)
        to_south = remote(field_a.at[pl.ds(first, 4)], north_a, 3, south)

        @pl.when(jnp.logical_not(is_top))
        def _():
            to_north.start()

        @pl.when(jnp.logical_not(is_bottom))
        def _():
            to_south.start()

        @pl.when(is_top)
        def _():
            for k in range(4):
                flip_a[k] = flip(field_a[top_slot - k])
            pltpu.make_async_remote_copy(
                src_ref=flip_a, dst_ref=north_a, send_sem=send_sem.at[2], recv_sem=recv_sem.at[3],
                device_id=mirror, device_id_type=MESH,
            ).start()

        base = base_ref[...]
        lat_frac = frac_ref[0:1, :]
        lon_frac = frac_ref[1:2, :]
        base_row = jnp.zeros_like(base)
        for j in range(1, rows):
            base_row = base_row + (base >= j * width).astype(jnp.int32)
        base_col = base - base_row * width
        zero_obs = jnp.zeros((1, n_obs), F32)

        def row_weight(j):
            return jnp.where(base_row == j, 1.0 - lat_frac, zero_obs) + jnp.where(
                base_row + 1 == j, lat_frac, zero_obs
            )

        row_weights = [row_weight(j) for j in range(rows + 1)]
        cell = lax.broadcasted_iota(jnp.int32, (width, n_obs), 0)
        col_weight = jnp.where(cell == base_col, 1.0 - lon_frac, 0.0) + jnp.where(
            cell == base_col + 1, lon_frac, 0.0
        )
        last_weight = jnp.where(base_col == width - 1, lon_frac, zero_obs)
        rim_low = (first + base_row) * 8
        rim_weight = jnp.where(cell == rim_low, (1.0 - lat_frac) * last_weight, 0.0) + jnp.where(
            cell == rim_low + 8, lat_frac * last_weight, 0.0
        )
        eof_pad[...] = jnp.zeros_like(eof_pad)
        eof_pad[0:levels, 0:levels] = eof_ref[...]
        rinv_pad[levels - levels % 8 : lp, :] = jnp.zeros((lp - (levels - levels % 8), n_obs), F32)
        rinv_pad[0:levels, :] = rinv_ref[...]
        eof_full = eof_pad[...]
        eof = eof_full[:lp, :lp]
        eof_t = eof_full.T[:lp, :lp]

        def second_leg(comb, flipc, cnorth, csouth, start):
            legs = (
                remote(comb, csouth, start, north),
                remote(comb, cnorth, start + 1, south),
                pltpu.make_async_remote_copy(
                    src_ref=flipc, dst_ref=cnorth, send_sem=send_sem.at[start],
                    recv_sem=recv_sem.at[start + 1], device_id=mirror, device_id_type=MESH,
                ),
            )

            @pl.when(jnp.logical_not(is_top))
            def _():
                legs[0].start()

            @pl.when(jnp.logical_not(is_bottom))
            def _():
                legs[1].start()

            @pl.when(is_top)
            def _():
                flipc[...] = flip_packed(comb[...])
                legs[2].start()

            return legs

        to_west.wait_recv()
        to_east.wait_recv()
        comb_a[...] = jnp.where(sub8 < 4, east_a[...], west_a[...])
        legs_a = second_leg(comb_a, flipc_a, cnorth_a, csouth_a, 4)

        @pl.when(is_bottom)
        def _():
            south_a[...] = jnp.zeros_like(south_a)
            csouth_a[...] = jnp.zeros_like(csouth_a)

        to_south.wait_recv()

        @pl.when(jnp.logical_not(is_bottom))
        def _():
            to_north.wait_recv()

        for k in range(4):
            field_a[after + k] = north_a[k]
        for k in range(3):
            field_a[first - 3 + k] = south_a[k]
        legs_a[1].wait_recv()

        @pl.when(jnp.logical_not(is_bottom))
        def _():
            legs_a[0].wait_recv()

        in_north = (lane >= after * 8 - 4) & (lane < (after + 4) * 8 - 4)
        in_south = (lane < first * 8 - 4) | (lane >= (after + 4) * 8 - 4)
        halo_a[...] = jnp.where(
            in_north, roll(cnorth_a[...], 64), jnp.where(in_south, roll(csouth_a[...], 64), comb_a[...])
        )

        low, high = first - 3, after + 3

        def shifted_rim(h, crossing):
            he = roll(jnp.where(lax.rem(lane[: h.shape[0]], 8) == 0, crossing, h), -1)
            hw = roll(jnp.where(lax.rem(lane[: h.shape[0]], 8) == 7, crossing, h), 1)
            return he, hw

        def crossing_of(rows_of, slots):
            out = None
            for e in slots:
                moved = roll(rows_of(e), e * 8)
                if out is None:
                    out = moved
                else:
                    at = lane[: moved.shape[0]]
                    out = jnp.where((at == e * 8) | (at == e * 8 - 1), moved, out)
            return out

        def shifted(v, rim, e):
            near = lane[: v.shape[0]]
            side = roll(rim, -e * 8)
            ve = roll(jnp.where(near == 0, side, v), -1)
            vw = roll(jnp.where(near == width - 1, side, v), 1)
            return ve, vw

        slots_all = range(low, high + 1)

        def level_row(ref_value, at):
            return ref_value[at : at + 1, :]

        h_all = halo_a[...]
        h_ke, h_kn, h_w = (level_row(h_all, at) for at in (ke_at, kn_at, wet_at))
        f_ke = {e: field_a[e, ke_at : ke_at + 1, :] for e in slots_all}
        f_kn = {e: field_a[e, kn_at : kn_at + 1, :] for e in slots_all}
        f_w = {e: field_a[e, wet_at : wet_at + 1, :] for e in slots_all}
        hw_east, _ = shifted_rim(h_w, crossing_of(lambda e: f_w[e], slots_all))
        hke_east, _ = shifted_rim(h_ke, crossing_of(lambda e: f_ke[e], slots_all))
        beyond = (lane1 >= after * 8 - 4) & is_top
        fold_row = (lane1 >= top_slot * 8 - 4) & (lane1 < after * 8 - 4) & is_top
        h_e = jnp.where(beyond, hke_east, h_ke) * h_w * hw_east
        kn_up = roll(h_kn, -8)
        h_n = jnp.where(beyond, kn_up, jnp.where(fold_row, 0.5 * (h_kn + kn_up), h_kn)) * h_w * roll(h_w, -8)
        face_e, face_n = {}, {}
        for e in slots_all:
            w_east, _ = shifted(f_w[e], h_w, e)
            ke = f_ke[e]
            if e >= after:
                ke = jnp.where(is_top, shifted(ke, h_ke, e)[0], ke)
            face_e[e] = ke * f_w[e] * w_east
            if e < high:
                kn = f_kn[e]
                if e >= after:
                    kn = jnp.where(is_top, f_kn[e + 1], kn)
                elif e == top_slot:
                    kn = jnp.where(is_top, 0.5 * (kn + f_kn[e + 1]), kn)
                face_n[e] = kn * f_w[e] * f_w[e + 1]
        _, h_west = shifted_rim(h_e, crossing_of(lambda e: face_e[e], slots_all))
        h_s = roll(h_n, 8)
        for k, value in enumerate((1.0 - h_e - h_west - h_n - h_s, h_e, h_west, h_n, h_s)):
            hcoef[k : k + 1, :] = value
        for e in range(low + 1, high):
            _, f_west = shifted(face_e[e], h_e, e)
            center = 1.0 - face_e[e] - f_west - face_n[e] - face_n[e - 1]
            for k, value in enumerate((center, face_e[e], f_west, face_n[e], face_n[e - 1])):
                coef[e, k : k + 1, :] = value

        def diffuse(src, dst, hsrc, hdst, lo, hi, rim=True):
            h = hsrc[...]
            if rim:
                crossing = crossing_of(lambda e: src[e], range(lo, hi + 1))
                he, hw = shifted_rim(h, crossing)
                hdst[...] = (
                    hcoef[0:1, :] * h + hcoef[1:2, :] * he + hcoef[2:3, :] * hw
                    + hcoef[3:4, :] * roll(h, -8) + hcoef[4:5, :] * roll(h, 8)
                )
            for e in range(lo, hi + 1):
                v = src[e]
                ve, vw = shifted(v, h, e)
                dst[e] = (
                    coef[e, 0:1, :] * v + coef[e, 1:2, :] * ve + coef[e, 2:3, :] * vw
                    + coef[e, 3:4, :] * src[e + 1] + coef[e, 4:5, :] * src[e - 1]
                )

        to_west.wait_send()
        to_east.wait_send()

        @pl.when(jnp.logical_not(is_top))
        def _():
            to_north.wait_send()
            legs_a[0].wait_send()

        @pl.when(jnp.logical_not(is_bottom))
        def _():
            to_south.wait_send()
            legs_a[1].wait_send()

        @pl.when(is_top)
        def _():
            pltpu.make_async_remote_copy(
                src_ref=flip_a, dst_ref=north_a, send_sem=send_sem.at[2], recv_sem=recv_sem.at[3],
                device_id=mirror, device_id_type=MESH,
            ).wait_send()
            legs_a[2].wait_send()

        diffuse(field_a, field_b, halo_a, halo_b, first - 2, after + 2)
        diffuse(field_b, field_a, halo_b, halo_a, first - 1, after + 1)
        diffuse(field_a, field_b, halo_a, halo_b, first, after)

        rim_used = (sub8 == 0) & (lane >= first * 8) & (lane <= after * 8)
        profile = mm(jnp.where(rim_used, halo_b[...], 0.0), rim_weight)
        for j in range(rows + 1):
            profile = profile + row_weights[j] * mm(field_b[first + j], col_weight)
        weighted = rinv_pad[...] * mm(eof, profile)
        back = mm(eof_t, weighted)

        for j in range(rows + 1):
            spread[j] = mm(row_weights[j] * back, col_weight, ((1,), (1,)))
        over = mm(back, rim_weight, ((1,), (1,)))
        own = packed(spread, range(first, after + 1), first)
        over_slots = (sub8 == 3) & (lane >= first * 8) & (lane <= after * 8 + 3)
        pack_b[...] = jnp.where(over_slots, roll(over, 3), jnp.where(sub8 == 4, 0.0, own))
        to_west_b = remote(pack_b, east_b, 6, west)
        to_east_b = remote(pack_b, west_b, 7, east)
        to_west_b.start()
        to_east_b.start()
        to_north_b = remote(spread.at[pl.ds(rows - 3, 4)], south_b, 8, north)
        to_south_b = remote(spread.at[pl.ds(0, 3)], north_b, 9, south)
        to_mirror_b = pltpu.make_async_remote_copy(
            src_ref=flip_b, dst_ref=north_b, send_sem=send_sem.at[8], recv_sem=recv_sem.at[9],
            device_id=mirror, device_id_type=MESH,
        )

        @pl.when(jnp.logical_not(is_top))
        def _():
            to_north_b.start()

        @pl.when(jnp.logical_not(is_bottom))
        def _():
            to_south_b.start()

        @pl.when(is_top)
        def _():
            for k in range(3):
                flip_b[k] = flip(spread[rows - 1 - k])
            to_mirror_b.start()

        to_west_b.wait_recv()
        to_east_b.wait_recv()
        comb_b[...] = jnp.where(sub8 < 3, east_b[...], west_b[...]) + jnp.where(sub8 == 0, over, 0.0)
        legs_b = second_leg(comb_b, flipc_b, cnorth_b, csouth_b, 10)

        @pl.when(is_bottom)
        def _():
            south_b[...] = jnp.zeros_like(south_b)
            csouth_b[...] = jnp.zeros_like(csouth_b)

        to_south_b.wait_recv()
        legs_b[1].wait_recv()

        @pl.when(jnp.logical_not(is_bottom))
        def _():
            to_north_b.wait_recv()
            legs_b[0].wait_recv()

        in_north_b = (lane >= after * 8 - 4) & (lane < (after + 3) * 8 - 4)
        in_south_b = (lane >= (first - 3) * 8 - 4) & (lane < (first + 1) * 8 - 4)
        rim = (
            comb_b[...] + jnp.where(in_north_b, roll(cnorth_b[...], 64), 0.0)
            + jnp.where(in_south_b, roll(csouth_b[...], 64), 0.0)
        )
        halo_a[...] = rim
        for e in range(first - 3, after + 3):
            if e < first:
                v = south_b[e - first + 3]
            elif e == first:
                v = spread[0] + south_b[3]
            elif e < after:
                v = spread[e - first]
            elif e == after:
                v = spread[rows] + north_b[0]
            else:
                v = north_b[e - after]
            v = v + jnp.where(lane == 0, roll(rim, -e * 8 - 3), 0.0)
            if e >= after:
                v = v + jnp.where(lane == width - 1, roll(rim, -e * 8 + 3), 0.0)
            field_a[e] = v

        diffuse(field_a, field_b, halo_a, halo_b, first - 2, after + 1)
        diffuse(field_b, field_a, halo_b, halo_a, first - 1, after)
        diffuse(field_a, field_b, halo_a, halo_b, first, after - 1, rim=False)

        sums = [jnp.zeros((levels, width), F32) for _ in range(4)]
        for j in range(rows):
            d = d_ref[:, j, :]
            r = r_ref[:, j, :]
            im = d + field_b[first + j, 0:levels, :]
            image[j, 0:levels, :] = im
            for k, term in enumerate((r * r, d * im, r * im, im * im)):
                sums[k] = sums[k] + term
        for k in range(4):
            red[k : k + 1, :] = jnp.sum(sums[k], axis=0, keepdims=True)
        red[4:8, :] = jnp.zeros((4, width), F32)

        def lon_copy(k):
            return pltpu.make_async_remote_copy(
                src_ref=red, dst_ref=lon_in.at[k], send_sem=lon_send.at[k], recv_sem=lon_recv.at[k],
                device_id=(lax.rem(lon + k, n_lon), lat), device_id_type=MESH,
            )

        def lat_copy(k):
            return pltpu.make_async_remote_copy(
                src_ref=red2, dst_ref=lat_in.at[k], send_sem=lat_send.at[k], recv_sem=lat_recv.at[k],
                device_id=(lon, lax.rem(lat + k, n_lat)), device_id_type=MESH,
            )

        for k in range(1, n_lon):
            lon_copy(k).start()
        total = red[...]
        for k in range(1, n_lon):
            lon_copy(k).wait_recv()
        for k in range(1, n_lon):
            total = total + lon_in[k]
        red2[...] = total
        for k in range(1, n_lat):
            lat_copy(k).start()
        for k in range(1, n_lat):
            lat_copy(k).wait_recv()
        for k in range(1, n_lat):
            total = total + lat_in[k]
        scalars = jnp.sum(total, axis=1, keepdims=True)
        old_norm = scalars[0:1]
        curvature = scalars[1:2]
        cross = scalars[2:3]
        square = scalars[3:4]
        step = old_norm / curvature
        new_norm = old_norm - 2.0 * (step * cross) + step * (step * square)
        ratio = new_norm / old_norm
        step_ref[...] = step
        for j in range(rows):
            nr = r_ref[:, j, :] - step * image[j, 0:levels, :]
            nr_ref[:, j, :] = nr
            nd_ref[:, j, :] = nr + ratio * d_ref[:, j, :]

        to_west_b.wait_send()
        to_east_b.wait_send()

        @pl.when(jnp.logical_not(is_top))
        def _():
            to_north_b.wait_send()
            legs_b[0].wait_send()

        @pl.when(jnp.logical_not(is_bottom))
        def _():
            to_south_b.wait_send()
            legs_b[1].wait_send()

        @pl.when(is_top)
        def _():
            to_mirror_b.wait_send()
            legs_b[2].wait_send()

        for k in range(1, n_lon):
            lon_copy(k).wait_send()
        for k in range(1, n_lat):
            lat_copy(k).wait_send()

    def tile(*lead):
        return pltpu.VMEM((*lead, lp, width), F32)

    ext = rows + 8
    scratch = [
        tile(ext), tile(ext), tile(), tile(), pltpu.VMEM((ext, 8, width), F32), pltpu.VMEM((8, width), F32),
        tile(), tile(), tile(), tile(), tile(4), tile(), tile(4), tile(3), tile(), tile(),
        tile(rows + 1), tile(), tile(), tile(), tile(), tile(3), tile(), tile(3), tile(4), tile(), tile(),
        pltpu.VMEM((width, width), F32), pltpu.VMEM((lp, n_obs), F32), tile(rows),
        pltpu.VMEM((8, width), F32), pltpu.VMEM((n_lon, 8, width), F32),
        pltpu.VMEM((8, width), F32), pltpu.VMEM((n_lat, 8, width), F32),
        pltpu.SemaphoreType.DMA((12,)), pltpu.SemaphoreType.DMA((12,)),
        pltpu.SemaphoreType.DMA((n_lon,)), pltpu.SemaphoreType.DMA((n_lon,)),
        pltpu.SemaphoreType.DMA((n_lat,)), pltpu.SemaphoreType.DMA((n_lat,)),
    ]
    vmem = pl.BlockSpec(memory_space=pltpu.VMEM)
    return pl.pallas_call(
        kernel,
        out_shape=(
            jax.ShapeDtypeStruct((levels, rows, width), F32),
            jax.ShapeDtypeStruct((levels, rows, width), F32),
            jax.ShapeDtypeStruct((1, 1), F32),
        ),
        in_specs=[vmem] * 9,
        out_specs=(vmem, vmem, vmem),
        scratch_shapes=scratch,
        compiler_params=pltpu.CompilerParams(
            collective_id=0, has_side_effects=True, vmem_limit_bytes=48 * 1024 * 1024
        ),
    )


def solution(mesh):
    n_lon, n_lat = mesh.shape["lon"], mesh.shape["lat"]

    def per_device(direction, residual, eof_basis, kappa_east, kappa_north, wet_mask, obs_base, obs_frac, obs_rinv):
        levels, rows, width = direction.shape
        n_obs = obs_base.shape[-1]
        call = make_kernel(n_lon, n_lat, levels, rows, width, n_obs)
        new_residual, new_direction, step = call(
            direction, residual, eof_basis, kappa_east, kappa_north, wet_mask,
            obs_base.reshape(1, n_obs), obs_frac.reshape(2, n_obs), obs_rinv.reshape(levels, n_obs),
        )
        return new_residual, new_direction, step.reshape(())

    return jax.shard_map(
        per_device,
        mesh=mesh,
        in_specs=(
            P(None, "lat", "lon"),
            P(None, "lat", "lon"),
            P(),
            P("lat", "lon"),
            P("lat", "lon"),
            P("lat", "lon"),
            P("lat", "lon", None),
            P(None, "lat", "lon", None),
            P(None, "lat", "lon", None),
        ),
        out_specs=(P(None, "lat", "lon"), P(None, "lat", "lon"), P()),
        check_vma=False,
    )
```

```python
import jax
import jax.numpy as jnp
from jax import lax
from jax.experimental import pallas as pl
from jax.experimental.pallas import tpu as pltpu
from jax.sharding import PartitionSpec as P

F32 = jnp.float32
MESH = pl.DeviceIdType.MESH


BF16 = jnp.bfloat16


def parts(x, count=2):
    out = []
    for _ in range(count):
        part = x.astype(BF16)
        out.append(part)
        x = x - part.astype(F32)
    return out


def mm(a, b, dims=((1,), (0,))):
    def one(x, y):
        return lax.dot_general(x, y, (dims, ((), ())), preferred_element_type=F32)

    return one(a[0], b[0]) + (one(a[0], b[1]) + one(a[1], b[0]))


def make_kernel(n_lon, n_lat, levels, rows, width, n_obs):
    padded_levels = -(-(levels + 3) // 8) * 8
    lp = padded_levels
    ke_at, kn_at, wet_at = levels, levels + 1, levels + 2
    first = 4
    top_slot = first + rows - 1
    after = first + rows

    def roll(x, shift):
        shift = shift % width
        return x if shift == 0 else pltpu.roll(x, shift, 1)

    pieces = n_obs // width
    pair = n_lon // 2
    n_peers = pair * n_lat
    everyone = [(2 * a, b) for a in range(pair) for b in range(n_lat) if a or b]
    if n_peers <= 32:
        phases = [everyone]
    else:
        phases = [[p for p in everyone if p[1] == 0], [p for p in everyone if p[0] == 0]]
    greeted = [(a, 0) for a in range(1, n_lon)] + [(0, b) for b in range(1, n_lat)]
    if len(phases) == 1:
        greeted += [p for p in everyone if p[0] and p[1]]
    n_copies = 1 + sum(len(p) for p in phases)

    def kernel(
        d_hbm, r_hbm, eof_hbm, ke_hbm, kn_hbm, wet_hbm, base_hbm, frac_hbm, rinv_hbm,
        nr_ref, nd_ref, step_ref,
        field_a, field_b, halo_a, halo_b, coef, hcoef,
        pack_a, east_a, west_a, comb_a, flip_a, flipc_a, north_a, south_a, cnorth_a, csouth_a,
        spread, pack_b, east_b, west_b, comb_b, flip_b, flipc_b, north_b, south_b, cnorth_b, csouth_b,
        eof_pad, rinv_pad, image, red, pair_in, sums_in, sums_in2,
        d_ref, r_ref, eof_ref, ke_ref, kn_ref, wet_ref, base_ref, frac_ref, rinv_ref,
        send_sem, recv_sem, red_send, red_recv, load_sem,
    ):
        lon = lax.axis_index("lon")
        lat = lax.axis_index("lat")
        is_top = lat == n_lat - 1
        is_bottom = lat == 0
        east = (lax.rem(lon + 1, n_lon), lat)
        west = (lax.rem(lon + n_lon - 1, n_lon), lat)
        mirror = (n_lon - 1 - lon, lat)
        north = (lon, lax.rem(lat + 1, n_lat))
        south = (lon, lax.rem(lat + n_lat - 1, n_lat))
        lane = lax.broadcasted_iota(jnp.int32, (lp, width), 1)
        lane1 = lane[:1]
        sub8 = lax.rem(lane, 8)

        barrier = pltpu.get_barrier_semaphore()
        for a, b in greeted:
            pl.semaphore_signal(
                barrier, inc=1, device_id=(lax.rem(lon + a, n_lon), lax.rem(lat + b, n_lat)), device_id_type=MESH
            )
        loads = [
            pltpu.make_async_copy(src, dst, load_sem.at[k])
            for k, (src, dst) in enumerate((
                (d_hbm, d_ref), (ke_hbm, ke_ref), (kn_hbm, kn_ref), (wet_hbm, wet_ref), (eof_hbm, eof_ref),
                (base_hbm, base_ref), (frac_hbm, frac_ref), (rinv_hbm, rinv_ref), (r_hbm, r_ref),
            ))
        ]
        for load in loads:
            load.start()
        for load in loads[:4]:
            load.wait()

        for j in range(rows):
            e = first + j
            field_a[e, 0:levels, :] = d_ref[:, j, :]
            field_a[e, ke_at : ke_at + 1, :] = ke_ref[j : j + 1, :]
            field_a[e, kn_at : kn_at + 1, :] = kn_ref[j : j + 1, :]
            field_a[e, wet_at : wet_at + 1, :] = wet_ref[j : j + 1, :].astype(F32)
            if lp > levels + 3:
                field_a[e, levels + 3 : lp, :] = jnp.zeros((lp - levels - 3, width), F32)

        def group(e):
            off = lane - e * 8
            return (off >= -4) & (off < 4)

        def packed(ref, slots, shift=0):
            out = jnp.zeros((lp, width), F32)
            for e in slots:
                out = jnp.where(group(e), roll(ref[e - shift], e * 8), out)
            return out

        row_id = lax.broadcasted_iota(jnp.int32, (width, width), 0)
        col_id = lax.broadcasted_iota(jnp.int32, (width, width), 1)
        reverse = (row_id + col_id == width - 1).astype(F32).astype(BF16)

        def flip(x):
            return sum(jnp.dot(part, reverse, preferred_element_type=F32) for part in parts(x, 3)[::-1])

        def flip_packed(x):
            return roll(flip(x), (2 * top_slot + 1) * 8 - 64 - width)

        def remote(src, dst, index, device):
            return pltpu.make_async_remote_copy(
                src_ref=src, dst_ref=dst, send_sem=send_sem.at[index], recv_sem=recv_sem.at[index],
                device_id=device, device_id_type=MESH,
            )

        pack_a[...] = packed(field_a, range(first, after))
        pl.semaphore_wait(barrier, len(greeted))

        to_west = remote(pack_a, east_a, 0, west)
        to_east = remote(pack_a, west_a, 1, east)
        to_west.start()
        to_east.start()
        to_north = remote(field_a.at[pl.ds(after - 3, 3)], south_a, 2, north)
        to_south = remote(field_a.at[pl.ds(first, 4)], north_a, 3, south)

        @pl.when(jnp.logical_not(is_top))
        def _():
            to_north.start()

        @pl.when(jnp.logical_not(is_bottom))
        def _():
            to_south.start()

        @pl.when(is_top)
        def _():
            for k in range(4):
                flip_a[k] = flip(field_a[top_slot - k])
            pltpu.make_async_remote_copy(
                src_ref=flip_a, dst_ref=north_a, send_sem=send_sem.at[2], recv_sem=recv_sem.at[3],
                device_id=mirror, device_id_type=MESH,
            ).start()

        for load in loads[4:8]:
            load.wait()
        base = jnp.concatenate([base_ref[k : k + 1, :] for k in range(pieces)], axis=1)
        lat_frac = jnp.concatenate([frac_ref[k : k + 1, :] for k in range(pieces)], axis=1)
        lon_frac = jnp.concatenate([frac_ref[pieces + k : pieces + k + 1, :] for k in range(pieces)], axis=1)
        base_row = jnp.zeros_like(base)
        for j in range(1, rows):
            base_row = base_row + (base >= j * width).astype(jnp.int32)
        base_col = base - base_row * width
        zero_obs = jnp.zeros((1, n_obs), F32)

        def row_weight(j):
            return jnp.where(base_row == j, 1.0 - lat_frac, zero_obs) + jnp.where(
                base_row + 1 == j, lat_frac, zero_obs
            )

        row_weights = [row_weight(j) for j in range(rows + 1)]
        cell = lax.broadcasted_iota(jnp.int32, (width, n_obs), 0)
        col_weight = jnp.where(cell == base_col, 1.0 - lon_frac, 0.0) + jnp.where(
            cell == base_col + 1, lon_frac, 0.0
        )
        last_weight = jnp.where(base_col == width - 1, lon_frac, zero_obs)
        rim_low = (first + base_row) * 8
        rim_weight = jnp.where(cell == rim_low, (1.0 - lat_frac) * last_weight, 0.0) + jnp.where(
            cell == rim_low + 8, lat_frac * last_weight, 0.0
        )
        eof_pad[...] = jnp.zeros_like(eof_pad)
        eof_pad[0:levels, 0:levels] = eof_ref[...]
        rinv_pad[levels - levels % 8 : lp, :] = jnp.zeros((lp - (levels - levels % 8), n_obs), F32)
        for k in range(pieces):
            rinv_pad[0:levels, k * width : (k + 1) * width] = rinv_ref[:, k, :]
        eof_full = eof_pad[...]
        eof = parts(eof_full[:lp, :lp])
        eof_t = parts(eof_full.T[:lp, :lp])
        col_parts = parts(col_weight)
        rim_parts = parts(rim_weight)

        def second_leg(comb, flipc, cnorth, csouth, start):
            legs = (
                remote(comb, csouth, start, north),
                remote(comb, cnorth, start + 1, south),
                pltpu.make_async_remote_copy(
                    src_ref=flipc, dst_ref=cnorth, send_sem=send_sem.at[start],
                    recv_sem=recv_sem.at[start + 1], device_id=mirror, device_id_type=MESH,
                ),
            )

            @pl.when(jnp.logical_not(is_top))
            def _():
                legs[0].start()

            @pl.when(jnp.logical_not(is_bottom))
            def _():
                legs[1].start()

            @pl.when(is_top)
            def _():
                flipc[...] = flip_packed(comb[...])
                legs[2].start()

            return legs

        to_west.wait_recv()
        to_east.wait_recv()
        comb_a[...] = jnp.where(sub8 < 4, east_a[...], west_a[...])
        legs_a = second_leg(comb_a, flipc_a, cnorth_a, csouth_a, 4)

        @pl.when(is_bottom)
        def _():
            south_a[...] = jnp.zeros_like(south_a)
            csouth_a[...] = jnp.zeros_like(csouth_a)

        to_south.wait_recv()

        @pl.when(jnp.logical_not(is_bottom))
        def _():
            to_north.wait_recv()

        for k in range(4):
            field_a[after + k] = north_a[k]
        for k in range(3):
            field_a[first - 3 + k] = south_a[k]
        legs_a[1].wait_recv()

        @pl.when(jnp.logical_not(is_bottom))
        def _():
            legs_a[0].wait_recv()

        in_north = (lane >= after * 8 - 4) & (lane < (after + 4) * 8 - 4)
        in_south = (lane < first * 8 - 4) | (lane >= (after + 4) * 8 - 4)
        halo_a[...] = jnp.where(
            in_north, roll(cnorth_a[...], 64), jnp.where(in_south, roll(csouth_a[...], 64), comb_a[...])
        )

        low, high = first - 3, after + 3

        def shifted_rim(h, crossing):
            he = roll(jnp.where(lax.rem(lane[: h.shape[0]], 8) == 0, crossing, h), -1)
            hw = roll(jnp.where(lax.rem(lane[: h.shape[0]], 8) == 7, crossing, h), 1)
            return he, hw

        def crossing_of(rows_of, slots):
            out = None
            for e in slots:
                moved = roll(rows_of(e), e * 8)
                if out is None:
                    out = moved
                else:
                    at = lane[: moved.shape[0]]
                    out = jnp.where((at == e * 8) | (at == e * 8 - 1), moved, out)
            return out

        def shifted(v, rim, e):
            near = lane[: v.shape[0]]
            side = roll(rim, -e * 8)
            ve = roll(jnp.where(near == 0, side, v), -1)
            vw = roll(jnp.where(near == width - 1, side, v), 1)
            return ve, vw

        slots_all = range(low, high + 1)

        def level_row(ref_value, at):
            return ref_value[at : at + 1, :]

        h_all = halo_a[...]
        h_ke, h_kn, h_w = (level_row(h_all, at) for at in (ke_at, kn_at, wet_at))
        f_ke = {e: field_a[e, ke_at : ke_at + 1, :] for e in slots_all}
        f_kn = {e: field_a[e, kn_at : kn_at + 1, :] for e in slots_all}
        f_w = {e: field_a[e, wet_at : wet_at + 1, :] for e in slots_all}
        hw_east, _ = shifted_rim(h_w, crossing_of(lambda e: f_w[e], slots_all))
        hke_east, _ = shifted_rim(h_ke, crossing_of(lambda e: f_ke[e], slots_all))
        beyond = (lane1 >= after * 8 - 4) & is_top
        fold_row = (lane1 >= top_slot * 8 - 4) & (lane1 < after * 8 - 4) & is_top
        h_e = jnp.where(beyond, hke_east, h_ke) * h_w * hw_east
        kn_up = roll(h_kn, -8)
        h_n = jnp.where(beyond, kn_up, jnp.where(fold_row, 0.5 * (h_kn + kn_up), h_kn)) * h_w * roll(h_w, -8)
        face_e, face_n = {}, {}
        for e in slots_all:
            w_east, _ = shifted(f_w[e], h_w, e)
            ke = f_ke[e]
            if e >= after:
                ke = jnp.where(is_top, shifted(ke, h_ke, e)[0], ke)
            face_e[e] = ke * f_w[e] * w_east
            if e < high:
                kn = f_kn[e]
                if e >= after:
                    kn = jnp.where(is_top, f_kn[e + 1], kn)
                elif e == top_slot:
                    kn = jnp.where(is_top, 0.5 * (kn + f_kn[e + 1]), kn)
                face_n[e] = kn * f_w[e] * f_w[e + 1]
        _, h_west = shifted_rim(h_e, crossing_of(lambda e: face_e[e], slots_all))
        h_s = roll(h_n, 8)
        for k, value in enumerate((1.0 - h_e - h_west - h_n - h_s, h_e, h_west, h_n, h_s)):
            hcoef[k : k + 1, :] = value
        for e in range(low + 1, high):
            _, f_west = shifted(face_e[e], h_e, e)
            center = 1.0 - face_e[e] - f_west - face_n[e] - face_n[e - 1]
            for k, value in enumerate((center, face_e[e], f_west, face_n[e], face_n[e - 1])):
                coef[e, k : k + 1, :] = value

        def diffuse(src, dst, hsrc, hdst, lo, hi, rim=True):
            h = hsrc[...]
            if rim:
                crossing = crossing_of(lambda e: src[e], range(lo, hi + 1))
                he, hw = shifted_rim(h, crossing)
                hdst[...] = (
                    hcoef[0:1, :] * h + hcoef[1:2, :] * he + hcoef[2:3, :] * hw
                    + hcoef[3:4, :] * roll(h, -8) + hcoef[4:5, :] * roll(h, 8)
                )
            for e in range(lo, hi + 1):
                v = src[e]
                ve, vw = shifted(v, h, e)
                dst[e] = (
                    coef[e, 0:1, :] * v + coef[e, 1:2, :] * ve + coef[e, 2:3, :] * vw
                    + coef[e, 3:4, :] * src[e + 1] + coef[e, 4:5, :] * src[e - 1]
                )

        to_west.wait_send()
        to_east.wait_send()

        @pl.when(jnp.logical_not(is_top))
        def _():
            to_north.wait_send()
            legs_a[0].wait_send()

        @pl.when(jnp.logical_not(is_bottom))
        def _():
            to_south.wait_send()
            legs_a[1].wait_send()

        @pl.when(is_top)
        def _():
            pltpu.make_async_remote_copy(
                src_ref=flip_a, dst_ref=north_a, send_sem=send_sem.at[2], recv_sem=recv_sem.at[3],
                device_id=mirror, device_id_type=MESH,
            ).wait_send()
            legs_a[2].wait_send()

        diffuse(field_a, field_b, halo_a, halo_b, first - 2, after + 2)
        diffuse(field_b, field_a, halo_b, halo_a, first - 1, after + 1)
        diffuse(field_a, field_b, halo_a, halo_b, first, after)

        rim_used = (sub8 == 0) & (lane >= first * 8) & (lane <= after * 8)
        profile = mm(parts(jnp.where(rim_used, halo_b[...], 0.0)), rim_parts)
        along = mm(parts(field_b[first : after + 1].reshape((rows + 1) * lp, width)), col_parts)
        for j in range(rows + 1):
            profile = profile + row_weights[j] * along[j * lp : (j + 1) * lp]
        weighted = rinv_pad[...] * mm(eof, parts(profile))
        back = mm(eof_t, parts(weighted))

        by_row = jnp.concatenate([row_weights[j] * back for j in range(rows + 1)], axis=0)
        spread[...] = mm(parts(by_row), col_parts, ((1,), (1,))).reshape(rows + 1, lp, width)
        over = mm(parts(back), rim_parts, ((1,), (1,)))
        own = packed(spread, range(first, after + 1), first)
        over_slots = (sub8 == 3) & (lane >= first * 8) & (lane <= after * 8 + 3)
        pack_b[...] = jnp.where(over_slots, roll(over, 3), jnp.where(sub8 == 4, 0.0, own))
        to_west_b = remote(pack_b, east_b, 6, west)
        to_east_b = remote(pack_b, west_b, 7, east)
        to_west_b.start()
        to_east_b.start()
        to_north_b = remote(spread.at[pl.ds(rows - 3, 4)], south_b, 8, north)
        to_south_b = remote(spread.at[pl.ds(0, 3)], north_b, 9, south)
        to_mirror_b = pltpu.make_async_remote_copy(
            src_ref=flip_b, dst_ref=north_b, send_sem=send_sem.at[8], recv_sem=recv_sem.at[9],
            device_id=mirror, device_id_type=MESH,
        )

        @pl.when(jnp.logical_not(is_top))
        def _():
            to_north_b.start()

        @pl.when(jnp.logical_not(is_bottom))
        def _():
            to_south_b.start()

        @pl.when(is_top)
        def _():
            for k in range(3):
                flip_b[k] = flip(spread[rows - 1 - k])
            to_mirror_b.start()

        to_west_b.wait_recv()
        to_east_b.wait_recv()
        comb_b[...] = jnp.where(sub8 < 3, east_b[...], west_b[...]) + jnp.where(sub8 == 0, over, 0.0)
        legs_b = second_leg(comb_b, flipc_b, cnorth_b, csouth_b, 10)

        @pl.when(is_bottom)
        def _():
            south_b[...] = jnp.zeros_like(south_b)
            csouth_b[...] = jnp.zeros_like(csouth_b)

        to_south_b.wait_recv()
        legs_b[1].wait_recv()

        @pl.when(jnp.logical_not(is_bottom))
        def _():
            to_north_b.wait_recv()
            legs_b[0].wait_recv()

        in_north_b = (lane >= after * 8 - 4) & (lane < (after + 3) * 8 - 4)
        in_south_b = (lane >= (first - 3) * 8 - 4) & (lane < (first + 1) * 8 - 4)
        rim = (
            comb_b[...] + jnp.where(in_north_b, roll(cnorth_b[...], 64), 0.0)
            + jnp.where(in_south_b, roll(csouth_b[...], 64), 0.0)
        )
        halo_a[...] = rim
        for e in range(first - 3, after + 3):
            if e < first:
                v = south_b[e - first + 3]
            elif e == first:
                v = spread[0] + south_b[3]
            elif e < after:
                v = spread[e - first]
            elif e == after:
                v = spread[rows] + north_b[0]
            else:
                v = north_b[e - after]
            v = v + jnp.where(lane == 0, roll(rim, -e * 8 - 3), 0.0)
            if e >= after:
                v = v + jnp.where(lane == width - 1, roll(rim, -e * 8 + 3), 0.0)
            field_a[e] = v

        diffuse(field_a, field_b, halo_a, halo_b, first - 2, after + 1)
        diffuse(field_b, field_a, halo_b, halo_a, first - 1, after)
        diffuse(field_a, field_b, halo_a, halo_b, first, after - 1, rim=False)

        loads[8].wait()
        sums = [jnp.zeros((levels, width), F32) for _ in range(4)]
        for j in range(rows):
            d = d_ref[:, j, :]
            r = r_ref[:, j, :]
            im = d + field_b[first + j, 0:levels, :]
            image[j, 0:levels, :] = im
            for k, term in enumerate((r * r, d * im, r * im, im * im)):
                sums[k] = sums[k] + term
        for k in range(4):
            red[k : k + 1, :] = jnp.sum(sums[k], axis=0, keepdims=True)
        red[4:8, :] = jnp.zeros((4, width), F32)

        with_pair = pltpu.make_async_remote_copy(
            src_ref=red, dst_ref=pair_in, send_sem=red_send.at[0], recv_sem=red_recv.at[0],
            device_id=(lon + 1 - 2 * lax.rem(lon, 2), lat), device_id_type=MESH,
        )
        with_pair.start()
        sent = [with_pair]
        with_pair.wait_recv()
        total = red[...] + pair_in[...]
        index = 1
        for number, peers in enumerate(phases):
            into = (sums_in, sums_in2)[number]
            if len(phases) == 1:
                slots, slot = n_peers, lax.div(lon, 2) * n_lat + lat
            else:
                slots, slot = (pair, lax.div(lon, 2)) if number == 0 else (n_lat, lat)
            into[slot] = total
            copies = []
            for a, b in peers:
                copies.append(pltpu.make_async_remote_copy(
                    src_ref=into.at[slot], dst_ref=into.at[slot],
                    send_sem=red_send.at[index], recv_sem=red_recv.at[index],
                    device_id=(lax.rem(lon + a, n_lon), lax.rem(lat + b, n_lat)), device_id_type=MESH,
                ))
                index += 1
            for copy in copies:
                copy.start()
            for copy in copies:
                copy.wait_recv()
            sent += copies
            total = into[0]
            for k in range(1, slots):
                total = total + into[k]
        scalars = jnp.sum(total, axis=1, keepdims=True)
        old_norm = scalars[0:1]
        curvature = scalars[1:2]
        cross = scalars[2:3]
        square = scalars[3:4]
        step = old_norm / curvature
        new_norm = old_norm - 2.0 * (step * cross) + step * (step * square)
        ratio = new_norm / old_norm
        step_ref[...] = step
        for j in range(rows):
            nr = r_ref[:, j, :] - step * image[j, 0:levels, :]
            nr_ref[:, j, :] = nr
            nd_ref[:, j, :] = nr + ratio * d_ref[:, j, :]

        to_west_b.wait_send()
        to_east_b.wait_send()

        @pl.when(jnp.logical_not(is_top))
        def _():
            to_north_b.wait_send()
            legs_b[0].wait_send()

        @pl.when(jnp.logical_not(is_bottom))
        def _():
            to_south_b.wait_send()
            legs_b[1].wait_send()

        @pl.when(is_top)
        def _():
            to_mirror_b.wait_send()
            legs_b[2].wait_send()

        for copy in sent:
            copy.wait_send()

    def tile(*lead):
        return pltpu.VMEM((*lead, lp, width), F32)

    ext = rows + 8
    scratch = [
        tile(ext), tile(ext), tile(), tile(), pltpu.VMEM((ext, 8, width), F32), pltpu.VMEM((8, width), F32),
        tile(), tile(), tile(), tile(), tile(4), tile(), tile(4), tile(3), tile(), tile(),
        tile(rows + 1), tile(), tile(), tile(), tile(), tile(3), tile(), tile(3), tile(4), tile(), tile(),
        pltpu.VMEM((width, width), F32), pltpu.VMEM((lp, n_obs), F32), tile(rows),
        pltpu.VMEM((8, width), F32), pltpu.VMEM((8, width), F32),
        pltpu.VMEM((n_peers if len(phases) == 1 else pair, 8, width), F32), pltpu.VMEM((n_lat, 8, width), F32),
        pltpu.VMEM((levels, rows, width), F32), pltpu.VMEM((levels, rows, width), F32),
        pltpu.VMEM((levels, levels), F32), pltpu.VMEM((rows, width), F32), pltpu.VMEM((rows, width), F32),
        pltpu.VMEM((rows, width), jnp.int32), pltpu.VMEM((pieces, width), jnp.int32),
        pltpu.VMEM((2 * pieces, width), F32), pltpu.VMEM((levels, pieces, width), F32),
        pltpu.SemaphoreType.DMA((12,)), pltpu.SemaphoreType.DMA((12,)),
        pltpu.SemaphoreType.DMA((n_copies,)), pltpu.SemaphoreType.DMA((n_copies,)),
        pltpu.SemaphoreType.DMA((9,)),
    ]
    vmem = pl.BlockSpec(memory_space=pltpu.VMEM)
    return pl.pallas_call(
        kernel,
        out_shape=(
            jax.ShapeDtypeStruct((levels, rows, width), F32),
            jax.ShapeDtypeStruct((levels, rows, width), F32),
            jax.ShapeDtypeStruct((1, 1), F32),
        ),
        in_specs=[pl.BlockSpec(memory_space=pltpu.HBM)] * 9,
        out_specs=(vmem, vmem, vmem),
        scratch_shapes=scratch,
        compiler_params=pltpu.CompilerParams(
            collective_id=0, has_side_effects=True, vmem_limit_bytes=64 * 1024 * 1024 - 128 * 1024
        ),
    )


def solution(mesh):
    n_lon, n_lat = mesh.shape["lon"], mesh.shape["lat"]

    def per_device(direction, residual, eof_basis, kappa_east, kappa_north, wet_mask, obs_base, obs_frac, obs_rinv):
        levels, rows, width = direction.shape
        n_obs = obs_base.shape[-1]
        call = make_kernel(n_lon, n_lat, levels, rows, width, n_obs)
        new_residual, new_direction, step = call(
            direction, residual, eof_basis, kappa_east, kappa_north, wet_mask,
            obs_base.reshape(n_obs // width, width), obs_frac.reshape(2 * n_obs // width, width),
            obs_rinv.reshape(levels, n_obs // width, width),
        )
        return new_residual, new_direction, step.reshape(())

    return jax.shard_map(
        per_device,
        mesh=mesh,
        in_specs=(
            P(None, "lat", "lon"),
            P(None, "lat", "lon"),
            P(),
            P("lat", "lon"),
            P("lat", "lon"),
            P("lat", "lon"),
            P("lat", "lon", None),
            P(None, "lat", "lon", None),
            P(None, "lat", "lon", None),
        ),
        out_specs=(P(None, "lat", "lon"), P(None, "lat", "lon"), P()),
        check_vma=False,
    )
```

```python
import jax
import jax.numpy as jnp
from jax import lax
from jax.experimental import pallas as pl
from jax.experimental.pallas import tpu as pltpu
from jax.sharding import PartitionSpec as P

F32 = jnp.float32
MESH = pl.DeviceIdType.MESH


BF16 = jnp.bfloat16


def parts(x, count=2):
    out = []
    for _ in range(count):
        part = x.astype(BF16)
        out.append(part)
        x = x - part.astype(F32)
    return out


def mm(a, b, dims=((1,), (0,))):
    def one(x, y):
        return lax.dot_general(x, y, (dims, ((), ())), preferred_element_type=F32)

    return one(a[0], b[0]) + (one(a[0], b[1]) + one(a[1], b[0]))


def make_kernel(n_lon, n_lat, levels, rows, width, n_obs):
    padded_levels = -(-(levels + 3) // 8) * 8
    lp = padded_levels
    ke_at, kn_at, wet_at = levels, levels + 1, levels + 2
    first = 4
    top_slot = first + rows - 1
    after = first + rows

    def roll(x, shift):
        shift = shift % width
        return x if shift == 0 else pltpu.roll(x, shift, 1)

    pieces = n_obs // width
    pair = n_lon // 2
    n_peers = pair * n_lat
    everyone = [(2 * a, b) for a in range(pair) for b in range(n_lat) if a or b]
    if n_peers <= 32:
        phases = [everyone]
    else:
        phases = [[p for p in everyone if p[1] == 0], [p for p in everyone if p[0] == 0]]
    greeted = [(a, 0) for a in range(1, n_lon)] + [(0, b) for b in range(1, n_lat)]
    if len(phases) == 1:
        greeted += [p for p in everyone if p[0] and p[1]]
    n_copies = 1 + sum(len(p) for p in phases)

    def kernel(
        d_hbm, r_hbm, eof_hbm, ke_hbm, kn_hbm, wet_hbm, base_hbm, frac_hbm, rinv_hbm,
        image_hbm, step_ref, ratio_ref,
        field_a, field_b, halo_a, halo_b, coef, hcoef,
        pack_a, east_a, west_a, comb_a, flip_a, flipc_a, north_a, south_a, cnorth_a, csouth_a,
        spread, pack_b, east_b, west_b, comb_b, flip_b, flipc_b, north_b, south_b, cnorth_b, csouth_b,
        eof_pad, rinv_pad, red, pair_in, sums_in, sums_in2,
        d_ref, r_ref, eof_ref, ke_ref, kn_ref, wet_ref, base_ref, frac_ref, rinv_ref,
        send_sem, recv_sem, red_send, red_recv, load_sem,
    ):
        lon = lax.axis_index("lon")
        lat = lax.axis_index("lat")
        is_top = lat == n_lat - 1
        is_bottom = lat == 0
        east = (lax.rem(lon + 1, n_lon), lat)
        west = (lax.rem(lon + n_lon - 1, n_lon), lat)
        mirror = (n_lon - 1 - lon, lat)
        north = (lon, lax.rem(lat + 1, n_lat))
        south = (lon, lax.rem(lat + n_lat - 1, n_lat))
        lane = lax.broadcasted_iota(jnp.int32, (lp, width), 1)
        lane1 = lane[:1]
        sub8 = lax.rem(lane, 8)

        barrier = pltpu.get_barrier_semaphore()
        for a, b in greeted:
            pl.semaphore_signal(
                barrier, inc=1, device_id=(lax.rem(lon + a, n_lon), lax.rem(lat + b, n_lat)), device_id_type=MESH
            )
        loads = [
            pltpu.make_async_copy(src, dst, load_sem.at[k])
            for k, (src, dst) in enumerate((
                (d_hbm, d_ref), (ke_hbm, ke_ref), (kn_hbm, kn_ref), (wet_hbm, wet_ref), (eof_hbm, eof_ref),
                (base_hbm, base_ref), (frac_hbm, frac_ref), (rinv_hbm, rinv_ref), (r_hbm, r_ref),
            ))
        ]
        for load in loads:
            load.start()
        for load in loads[:4]:
            load.wait()

        for j in range(rows):
            e = first + j
            field_a[e, 0:levels, :] = d_ref[:, j, :]
            field_a[e, ke_at : ke_at + 1, :] = ke_ref[j : j + 1, :]
            field_a[e, kn_at : kn_at + 1, :] = kn_ref[j : j + 1, :]
            field_a[e, wet_at : wet_at + 1, :] = wet_ref[j : j + 1, :].astype(F32)
            if lp > levels + 3:
                field_a[e, levels + 3 : lp, :] = jnp.zeros((lp - levels - 3, width), F32)

        def group(e):
            off = lane - e * 8
            return (off >= -4) & (off < 4)

        def packed(ref, slots, shift=0):
            out = jnp.zeros((lp, width), F32)
            for e in slots:
                out = jnp.where(group(e), roll(ref[e - shift], e * 8), out)
            return out

        row_id = lax.broadcasted_iota(jnp.int32, (width, width), 0)
        col_id = lax.broadcasted_iota(jnp.int32, (width, width), 1)
        reverse = (row_id + col_id == width - 1).astype(F32).astype(BF16)

        def flip(x):
            return sum(jnp.dot(part, reverse, preferred_element_type=F32) for part in parts(x, 3)[::-1])

        def flip_packed(x):
            return roll(flip(x), (2 * top_slot + 1) * 8 - 64 - width)

        def remote(src, dst, index, device):
            return pltpu.make_async_remote_copy(
                src_ref=src, dst_ref=dst, send_sem=send_sem.at[index], recv_sem=recv_sem.at[index],
                device_id=device, device_id_type=MESH,
            )

        pack_a[...] = packed(field_a, range(first, after))
        pl.semaphore_wait(barrier, len(greeted))

        to_west = remote(pack_a, east_a, 0, west)
        to_east = remote(pack_a, west_a, 1, east)
        to_west.start()
        to_east.start()
        to_north = remote(field_a.at[pl.ds(after - 3, 3)], south_a, 2, north)
        to_south = remote(field_a.at[pl.ds(first, 4)], north_a, 3, south)

        @pl.when(jnp.logical_not(is_top))
        def _():
            to_north.start()

        @pl.when(jnp.logical_not(is_bottom))
        def _():
            to_south.start()

        @pl.when(is_top)
        def _():
            for k in range(4):
                flip_a[k] = flip(field_a[top_slot - k])
            pltpu.make_async_remote_copy(
                src_ref=flip_a, dst_ref=north_a, send_sem=send_sem.at[2], recv_sem=recv_sem.at[3],
                device_id=mirror, device_id_type=MESH,
            ).start()

        for load in loads[4:8]:
            load.wait()
        base = jnp.concatenate([base_ref[k : k + 1, :] for k in range(pieces)], axis=1)
        lat_frac = jnp.concatenate([frac_ref[k : k + 1, :] for k in range(pieces)], axis=1)
        lon_frac = jnp.concatenate([frac_ref[pieces + k : pieces + k + 1, :] for k in range(pieces)], axis=1)
        base_row = jnp.zeros_like(base)
        for j in range(1, rows):
            base_row = base_row + (base >= j * width).astype(jnp.int32)
        base_col = base - base_row * width
        zero_obs = jnp.zeros((1, n_obs), F32)

        def row_weight(j):
            return jnp.where(base_row == j, 1.0 - lat_frac, zero_obs) + jnp.where(
                base_row + 1 == j, lat_frac, zero_obs
            )

        row_weights = [row_weight(j) for j in range(rows + 1)]
        cell = lax.broadcasted_iota(jnp.int32, (width, n_obs), 0)
        col_weight = jnp.where(cell == base_col, 1.0 - lon_frac, 0.0) + jnp.where(
            cell == base_col + 1, lon_frac, 0.0
        )
        last_weight = jnp.where(base_col == width - 1, lon_frac, zero_obs)
        rim_low = (first + base_row) * 8
        rim_weight = jnp.where(cell == rim_low, (1.0 - lat_frac) * last_weight, 0.0) + jnp.where(
            cell == rim_low + 8, lat_frac * last_weight, 0.0
        )
        eof_pad[...] = jnp.zeros_like(eof_pad)
        eof_pad[0:levels, 0:levels] = eof_ref[...]
        rinv_pad[levels - levels % 8 : lp, :] = jnp.zeros((lp - (levels - levels % 8), n_obs), F32)
        for k in range(pieces):
            rinv_pad[0:levels, k * width : (k + 1) * width] = rinv_ref[:, k, :]
        eof_full = eof_pad[...]
        eof = parts(eof_full[:lp, :lp])
        eof_t = parts(eof_full.T[:lp, :lp])
        col_parts = parts(col_weight)
        rim_parts = parts(rim_weight)

        def second_leg(comb, flipc, cnorth, csouth, start):
            legs = (
                remote(comb, csouth, start, north),
                remote(comb, cnorth, start + 1, south),
                pltpu.make_async_remote_copy(
                    src_ref=flipc, dst_ref=cnorth, send_sem=send_sem.at[start],
                    recv_sem=recv_sem.at[start + 1], device_id=mirror, device_id_type=MESH,
                ),
            )

            @pl.when(jnp.logical_not(is_top))
            def _():
                legs[0].start()

            @pl.when(jnp.logical_not(is_bottom))
            def _():
                legs[1].start()

            @pl.when(is_top)
            def _():
                flipc[...] = flip_packed(comb[...])
                legs[2].start()

            return legs

        to_west.wait_recv()
        to_east.wait_recv()
        comb_a[...] = jnp.where(sub8 < 4, east_a[...], west_a[...])
        legs_a = second_leg(comb_a, flipc_a, cnorth_a, csouth_a, 4)

        @pl.when(is_bottom)
        def _():
            south_a[...] = jnp.zeros_like(south_a)
            csouth_a[...] = jnp.zeros_like(csouth_a)

        to_south.wait_recv()

        @pl.when(jnp.logical_not(is_bottom))
        def _():
            to_north.wait_recv()

        for k in range(4):
            field_a[after + k] = north_a[k]
        for k in range(3):
            field_a[first - 3 + k] = south_a[k]
        legs_a[1].wait_recv()

        @pl.when(jnp.logical_not(is_bottom))
        def _():
            legs_a[0].wait_recv()

        in_north = (lane >= after * 8 - 4) & (lane < (after + 4) * 8 - 4)
        in_south = (lane < first * 8 - 4) | (lane >= (after + 4) * 8 - 4)
        halo_a[...] = jnp.where(
            in_north, roll(cnorth_a[...], 64), jnp.where(in_south, roll(csouth_a[...], 64), comb_a[...])
        )

        low, high = first - 3, after + 3

        def shifted_rim(h, crossing):
            he = roll(jnp.where(lax.rem(lane[: h.shape[0]], 8) == 0, crossing, h), -1)
            hw = roll(jnp.where(lax.rem(lane[: h.shape[0]], 8) == 7, crossing, h), 1)
            return he, hw

        def crossing_of(rows_of, slots):
            out = None
            for e in slots:
                moved = roll(rows_of(e), e * 8)
                if out is None:
                    out = moved
                else:
                    at = lane[: moved.shape[0]]
                    out = jnp.where((at == e * 8) | (at == e * 8 - 1), moved, out)
            return out

        def shifted(v, rim, e):
            near = lane[: v.shape[0]]
            side = roll(rim, -e * 8)
            ve = roll(jnp.where(near == 0, side, v), -1)
            vw = roll(jnp.where(near == width - 1, side, v), 1)
            return ve, vw

        slots_all = range(low, high + 1)

        def level_row(ref_value, at):
            return ref_value[at : at + 1, :]

        h_all = halo_a[...]
        h_ke, h_kn, h_w = (level_row(h_all, at) for at in (ke_at, kn_at, wet_at))
        f_ke = {e: field_a[e, ke_at : ke_at + 1, :] for e in slots_all}
        f_kn = {e: field_a[e, kn_at : kn_at + 1, :] for e in slots_all}
        f_w = {e: field_a[e, wet_at : wet_at + 1, :] for e in slots_all}
        hw_east, _ = shifted_rim(h_w, crossing_of(lambda e: f_w[e], slots_all))
        hke_east, _ = shifted_rim(h_ke, crossing_of(lambda e: f_ke[e], slots_all))
        beyond = (lane1 >= after * 8 - 4) & is_top
        fold_row = (lane1 >= top_slot * 8 - 4) & (lane1 < after * 8 - 4) & is_top
        h_e = jnp.where(beyond, hke_east, h_ke) * h_w * hw_east
        kn_up = roll(h_kn, -8)
        h_n = jnp.where(beyond, kn_up, jnp.where(fold_row, 0.5 * (h_kn + kn_up), h_kn)) * h_w * roll(h_w, -8)
        face_e, face_n = {}, {}
        for e in slots_all:
            w_east, _ = shifted(f_w[e], h_w, e)
            ke = f_ke[e]
            if e >= after:
                ke = jnp.where(is_top, shifted(ke, h_ke, e)[0], ke)
            face_e[e] = ke * f_w[e] * w_east
            if e < high:
                kn = f_kn[e]
                if e >= after:
                    kn = jnp.where(is_top, f_kn[e + 1], kn)
                elif e == top_slot:
                    kn = jnp.where(is_top, 0.5 * (kn + f_kn[e + 1]), kn)
                face_n[e] = kn * f_w[e] * f_w[e + 1]
        _, h_west = shifted_rim(h_e, crossing_of(lambda e: face_e[e], slots_all))
        h_s = roll(h_n, 8)
        for k, value in enumerate((1.0 - h_e - h_west - h_n - h_s, h_e, h_west, h_n, h_s)):
            hcoef[k : k + 1, :] = value
        for e in range(low + 1, high):
            _, f_west = shifted(face_e[e], h_e, e)
            center = 1.0 - face_e[e] - f_west - face_n[e] - face_n[e - 1]
            for k, value in enumerate((center, face_e[e], f_west, face_n[e], face_n[e - 1])):
                coef[e, k : k + 1, :] = value

        def diffuse(src, dst, hsrc, hdst, lo, hi, rim=True):
            h = hsrc[...]
            if rim:
                crossing = crossing_of(lambda e: src[e], range(lo, hi + 1))
                he, hw = shifted_rim(h, crossing)
                hdst[...] = (
                    hcoef[0:1, :] * h + hcoef[1:2, :] * he + hcoef[2:3, :] * hw
                    + hcoef[3:4, :] * roll(h, -8) + hcoef[4:5, :] * roll(h, 8)
                )
            for e in range(lo, hi + 1):
                v = src[e]
                ve, vw = shifted(v, h, e)
                dst[e] = (
                    coef[e, 0:1, :] * v + coef[e, 1:2, :] * ve + coef[e, 2:3, :] * vw
                    + coef[e, 3:4, :] * src[e + 1] + coef[e, 4:5, :] * src[e - 1]
                )

        to_west.wait_send()
        to_east.wait_send()

        @pl.when(jnp.logical_not(is_top))
        def _():
            to_north.wait_send()
            legs_a[0].wait_send()

        @pl.when(jnp.logical_not(is_bottom))
        def _():
            to_south.wait_send()
            legs_a[1].wait_send()

        @pl.when(is_top)
        def _():
            pltpu.make_async_remote_copy(
                src_ref=flip_a, dst_ref=north_a, send_sem=send_sem.at[2], recv_sem=recv_sem.at[3],
                device_id=mirror, device_id_type=MESH,
            ).wait_send()
            legs_a[2].wait_send()

        diffuse(field_a, field_b, halo_a, halo_b, first - 2, after + 2)
        diffuse(field_b, field_a, halo_b, halo_a, first - 1, after + 1)
        diffuse(field_a, field_b, halo_a, halo_b, first, after)

        rim_used = (sub8 == 0) & (lane >= first * 8) & (lane <= after * 8)
        profile = mm(parts(jnp.where(rim_used, halo_b[...], 0.0)), rim_parts)
        along = mm(parts(field_b[first : after + 1].reshape((rows + 1) * lp, width)), col_parts)
        for j in range(rows + 1):
            profile = profile + row_weights[j] * along[j * lp : (j + 1) * lp]
        weighted = rinv_pad[...] * mm(eof, parts(profile))
        back = mm(eof_t, parts(weighted))

        by_row = jnp.concatenate([row_weights[j] * back for j in range(rows + 1)], axis=0)
        spread[...] = mm(parts(by_row), col_parts, ((1,), (1,))).reshape(rows + 1, lp, width)
        over = mm(parts(back), rim_parts, ((1,), (1,)))
        own = packed(spread, range(first, after + 1), first)
        over_slots = (sub8 == 3) & (lane >= first * 8) & (lane <= after * 8 + 3)
        pack_b[...] = jnp.where(over_slots, roll(over, 3), jnp.where(sub8 == 4, 0.0, own))
        to_west_b = remote(pack_b, east_b, 6, west)
        to_east_b = remote(pack_b, west_b, 7, east)
        to_west_b.start()
        to_east_b.start()
        to_north_b = remote(spread.at[pl.ds(rows - 3, 4)], south_b, 8, north)
        to_south_b = remote(spread.at[pl.ds(0, 3)], north_b, 9, south)
        to_mirror_b = pltpu.make_async_remote_copy(
            src_ref=flip_b, dst_ref=north_b, send_sem=send_sem.at[8], recv_sem=recv_sem.at[9],
            device_id=mirror, device_id_type=MESH,
        )

        @pl.when(jnp.logical_not(is_top))
        def _():
            to_north_b.start()

        @pl.when(jnp.logical_not(is_bottom))
        def _():
            to_south_b.start()

        @pl.when(is_top)
        def _():
            for k in range(3):
                flip_b[k] = flip(spread[rows - 1 - k])
            to_mirror_b.start()

        to_west_b.wait_recv()
        to_east_b.wait_recv()
        comb_b[...] = jnp.where(sub8 < 3, east_b[...], west_b[...]) + jnp.where(sub8 == 0, over, 0.0)
        legs_b = second_leg(comb_b, flipc_b, cnorth_b, csouth_b, 10)

        @pl.when(is_bottom)
        def _():
            south_b[...] = jnp.zeros_like(south_b)
            csouth_b[...] = jnp.zeros_like(csouth_b)

        to_south_b.wait_recv()
        legs_b[1].wait_recv()

        @pl.when(jnp.logical_not(is_bottom))
        def _():
            to_north_b.wait_recv()
            legs_b[0].wait_recv()

        in_north_b = (lane >= after * 8 - 4) & (lane < (after + 3) * 8 - 4)
        in_south_b = (lane >= (first - 3) * 8 - 4) & (lane < (first + 1) * 8 - 4)
        rim = (
            comb_b[...] + jnp.where(in_north_b, roll(cnorth_b[...], 64), 0.0)
            + jnp.where(in_south_b, roll(csouth_b[...], 64), 0.0)
        )
        halo_a[...] = rim
        for e in range(first - 3, after + 3):
            if e < first:
                v = south_b[e - first + 3]
            elif e == first:
                v = spread[0] + south_b[3]
            elif e < after:
                v = spread[e - first]
            elif e == after:
                v = spread[rows] + north_b[0]
            else:
                v = north_b[e - after]
            v = v + jnp.where(lane == 0, roll(rim, -e * 8 - 3), 0.0)
            if e >= after:
                v = v + jnp.where(lane == width - 1, roll(rim, -e * 8 + 3), 0.0)
            field_a[e] = v

        diffuse(field_a, field_b, halo_a, halo_b, first - 2, after + 1)
        diffuse(field_b, field_a, halo_b, halo_a, first - 1, after)
        diffuse(field_a, field_b, halo_a, halo_b, first, after - 1, rim=False)

        loads[8].wait()
        sums = [jnp.zeros((levels, width), F32) for _ in range(4)]
        for j in range(rows):
            d = d_ref[:, j, :]
            r = r_ref[:, j, :]
            im = d + field_b[first + j, 0:levels, :]
            r_ref[:, j, :] = im
            for k, term in enumerate((r * r, d * im, r * im, im * im)):
                sums[k] = sums[k] + term
        store = pltpu.make_async_copy(r_ref, image_hbm, load_sem.at[9])
        store.start()
        for k in range(4):
            red[k : k + 1, :] = jnp.sum(sums[k], axis=0, keepdims=True)
        red[4:8, :] = jnp.zeros((4, width), F32)

        with_pair = pltpu.make_async_remote_copy(
            src_ref=red, dst_ref=pair_in, send_sem=red_send.at[0], recv_sem=red_recv.at[0],
            device_id=(lon + 1 - 2 * lax.rem(lon, 2), lat), device_id_type=MESH,
        )
        with_pair.start()
        sent = [with_pair]
        with_pair.wait_recv()
        total = red[...] + pair_in[...]
        index = 1
        for number, peers in enumerate(phases):
            into = (sums_in, sums_in2)[number]
            if len(phases) == 1:
                slots, slot = n_peers, lax.div(lon, 2) * n_lat + lat
            else:
                slots, slot = (pair, lax.div(lon, 2)) if number == 0 else (n_lat, lat)
            into[slot] = total
            copies = []
            for a, b in peers:
                copies.append(pltpu.make_async_remote_copy(
                    src_ref=into.at[slot], dst_ref=into.at[slot],
                    send_sem=red_send.at[index], recv_sem=red_recv.at[index],
                    device_id=(lax.rem(lon + a, n_lon), lax.rem(lat + b, n_lat)), device_id_type=MESH,
                ))
                index += 1
            for copy in copies:
                copy.start()
            for copy in copies:
                copy.wait_recv()
            sent += copies
            total = into[0]
            for k in range(1, slots):
                total = total + into[k]
        scalars = jnp.sum(total, axis=1, keepdims=True)
        old_norm = scalars[0:1]
        curvature = scalars[1:2]
        cross = scalars[2:3]
        square = scalars[3:4]
        step = old_norm / curvature
        new_norm = old_norm - 2.0 * (step * cross) + step * (step * square)
        ratio = new_norm / old_norm
        step_ref[...] = step
        ratio_ref[...] = ratio
        store.wait()

        to_west_b.wait_send()
        to_east_b.wait_send()

        @pl.when(jnp.logical_not(is_top))
        def _():
            to_north_b.wait_send()
            legs_b[0].wait_send()

        @pl.when(jnp.logical_not(is_bottom))
        def _():
            to_south_b.wait_send()
            legs_b[1].wait_send()

        @pl.when(is_top)
        def _():
            to_mirror_b.wait_send()
            legs_b[2].wait_send()

        for copy in sent:
            copy.wait_send()

    def tile(*lead):
        return pltpu.VMEM((*lead, lp, width), F32)

    ext = rows + 8
    scratch = [
        tile(ext), tile(ext), tile(), tile(), pltpu.VMEM((ext, 8, width), F32), pltpu.VMEM((8, width), F32),
        tile(), tile(), tile(), tile(), tile(4), tile(), tile(4), tile(3), tile(), tile(),
        tile(rows + 1), tile(), tile(), tile(), tile(), tile(3), tile(), tile(3), tile(4), tile(), tile(),
        pltpu.VMEM((width, width), F32), pltpu.VMEM((lp, n_obs), F32),
        pltpu.VMEM((8, width), F32), pltpu.VMEM((8, width), F32),
        pltpu.VMEM((n_peers if len(phases) == 1 else pair, 8, width), F32), pltpu.VMEM((n_lat, 8, width), F32),
        pltpu.VMEM((levels, rows, width), F32), pltpu.VMEM((levels, rows, width), F32),
        pltpu.VMEM((levels, levels), F32), pltpu.VMEM((rows, width), F32), pltpu.VMEM((rows, width), F32),
        pltpu.VMEM((rows, width), jnp.int32), pltpu.VMEM((pieces, width), jnp.int32),
        pltpu.VMEM((2 * pieces, width), F32), pltpu.VMEM((levels, pieces, width), F32),
        pltpu.SemaphoreType.DMA((12,)), pltpu.SemaphoreType.DMA((12,)),
        pltpu.SemaphoreType.DMA((n_copies,)), pltpu.SemaphoreType.DMA((n_copies,)),
        pltpu.SemaphoreType.DMA((10,)),
    ]
    vmem = pl.BlockSpec(memory_space=pltpu.VMEM)
    return pl.pallas_call(
        kernel,
        out_shape=(
            jax.ShapeDtypeStruct((levels, rows, width), F32),
            jax.ShapeDtypeStruct((1, 1), F32),
            jax.ShapeDtypeStruct((1, 1), F32),
        ),
        in_specs=[pl.BlockSpec(memory_space=pltpu.HBM)] * 9,
        out_specs=(pl.BlockSpec(memory_space=pltpu.HBM), vmem, vmem),
        scratch_shapes=scratch,
        compiler_params=pltpu.CompilerParams(
            collective_id=0, has_side_effects=True, vmem_limit_bytes=64 * 1024 * 1024 - 128 * 1024
        ),
    )


def solution(mesh):
    n_lon, n_lat = mesh.shape["lon"], mesh.shape["lat"]

    def per_device(direction, residual, eof_basis, kappa_east, kappa_north, wet_mask, obs_base, obs_frac, obs_rinv):
        levels, rows, width = direction.shape
        n_obs = obs_base.shape[-1]
        call = make_kernel(n_lon, n_lat, levels, rows, width, n_obs)
        image, step, ratio = call(
            direction, residual, eof_basis, kappa_east, kappa_north, wet_mask,
            obs_base.reshape(n_obs // width, width), obs_frac.reshape(2 * n_obs // width, width),
            obs_rinv.reshape(levels, n_obs // width, width),
        )
        step = step.reshape(())
        new_residual = residual - step * image
        new_direction = new_residual + ratio.reshape(()) * direction
        return new_residual, new_direction, step

    return jax.shard_map(
        per_device,
        mesh=mesh,
        in_specs=(
            P(None, "lat", "lon"),
            P(None, "lat", "lon"),
            P(),
            P("lat", "lon"),
            P("lat", "lon"),
            P("lat", "lon"),
            P("lat", "lon", None),
            P(None, "lat", "lon", None),
            P(None, "lat", "lon", None),
        ),
        out_specs=(P(None, "lat", "lon"), P(None, "lat", "lon"), P()),
        check_vma=False,
    )
```
